32 devices in a mesh: ctx: 8 (over z, y), tp: 4 (over x, core).
Axes of the slice: x: 2, y: 2, z: 4, core: 2. Of those that a mesh axis runs over, the one named last changes fastest.
Arguments:
- queries: bfloat16 [12288, 8192], P('ctx', 'tp'), may hold values from -6 to 6
- keys: bfloat16 [12288, 8192], P('ctx', 'tp'), may hold values from -6 to 6
- values: bfloat16 [12288, 8192], P('ctx', 'tp'), may hold values from -180 to 180
- gain: float32 [8192], P('tp'), may hold values from 0.5 to 1.5
- starts: int32 [12288], P('ctx'), may hold values 0 or 1
- source_unit: int32 [128], replicated, may hold values from 0 to 127, as said below
Outputs:
- normed: bfloat16 [12288, 8192], P('ctx', 'tp')
The draws below stay inside these ranges and needn't reach their ends.
Inputs may be any that keep to these rules, and one draw needn't show every extreme that they name: `source_unit`: A permutation of the units. The units of ctx index b are balanced units 2 * 8 * b to 2 * 8 * b + 2 * 8 - 1, and exactly 2 of them come from the units of each arrival index a (arrival units 2 * 8 * a to 2 * 8 * a + 2 * 8 - 1).
All inputs are finite; a program needn't handle non-finite values. No bound on the sum of `starts` on one device may be relied on, other than what follows from the above.
Results may differ from the reference program's by a relative error of at most 0.0053.
Values may be sent and summed in bfloat16 or wider, within the bound.
A program may use at most 128 MiB of HBM per device.

```python
import math
import jax
import jax.numpy as jnp
from jax import lax

HEADS = 64
DH = 128
TOK_DEV = 1536
TOKENS = 12288
UNIT = 96
BLK = 768
N_CTX = 8


def draw_values(key, part):
    first_key, second_key = jax.random.split(key)
    head_pos = jnp.arange(HEADS, dtype=jnp.float32)
    rising = jnp.repeat(3.0 ** (head_pos / (HEADS - 1)), DH)
    row_scale = jnp.exp(jax.random.uniform(second_key, (TOKENS, 1), minval=0.0, maxval=math.log(10.0)))
    base = jnp.clip(jax.random.normal(first_key, (TOKENS, HEADS * DH)), -6.0, 6.0)
    return jnp.clip(base * row_scale * rising[None, :], -180.0, 180.0).astype(jnp.bfloat16)


def draw_source_unit(key, part):
    shard_count = N_CTX
    slot_count = 2 * N_CTX
    key_send, key_recv = jax.random.split(key, 2)
    offset_list = jnp.repeat(jnp.arange(shard_count, dtype=jnp.int32), 2, total_repeat_length=slot_count)
    send_order = jax.vmap(lambda single: jax.random.permutation(single, slot_count))(jax.random.split(key_send, shard_count))
    recv_order = jax.vmap(lambda single: jax.random.permutation(single, slot_count))(jax.random.split(key_recv, shard_count))
    target = jnp.arange(shard_count, dtype=jnp.int32)[:, None]
    position = jnp.arange(slot_count, dtype=jnp.int32)[None, :]
    source = (target - offset_list[None, :]) % shard_count
    source_slot = send_order[source, jnp.broadcast_to(position, source.shape)]
    entry = (source * slot_count + source_slot).astype(jnp.int32)
    table = jnp.zeros((shard_count, slot_count), jnp.int32)
    table = table.at[jnp.broadcast_to(target, source.shape), recv_order].set(entry)
    return table.reshape(-1)


def place_ends(values, rng, smallest, top_value):
    shape = values.shape
    spot = [jax.random.randint(jax.random.fold_in(rng, axis), (), 0, shape[axis]) for axis in range(len(shape))]
    values = values.at[tuple(spot)].set(smallest)
    longest = shape.index(max(shape))
    spot[longest] = (spot[longest] + 1) % shape[longest]
    return values.at[tuple(spot)].set(top_value)


def block_scale(stream_key, shape, cuts, least, largest):
    def one(axis_at, blocks):
        steps = jax.random.uniform(jax.random.fold_in(jax.random.fold_in(stream_key, 6), axis_at), (blocks,), jnp.float32, least / len(cuts), largest / len(cuts))
        return jnp.repeat(jnp.exp(steps), shape[axis_at] // blocks).reshape((-1,) + (1,) * (len(shape) - axis_at - 1))

    level = one(*cuts[0])
    for cut in cuts[1:]:
        level = level * one(*cut)
    return level


def scatter_about(stream_key, dims, scale, reach, cuts=(), kind=jnp.bfloat16):
    factor_of = block_scale(stream_key, dims, cuts, -0.22, 0.18) if cuts else 1.0
    values = jax.random.normal(stream_key, dims, jnp.float32) * scale * factor_of
    return jnp.minimum(jnp.maximum(values, -reach), reach).astype(kind)


def setup_inputs(seed: int = 0) -> dict:
    key_of = jax.random.split(jax.random.key(seed), 7)
    queries = scatter_about(key_of[0], (TOKENS, HEADS * DH), 1.0, 6.0, ((0, 8), (1, 4)))
    keys = scatter_about(key_of[1], (TOKENS, HEADS * DH), 1.0, 6.0, ((0, 8), (1, 4)))
    values = draw_values(jax.random.fold_in(key_of[6], 71), 0)
    gain = jnp.clip(1.0 + 0.1 * jax.random.normal(key_of[3], (HEADS * DH,), jnp.float32), 0.5, 1.5)
    starts = place_ends((jax.random.randint(key_of[4], (TOKENS,), 0, 2 * TOK_DEV) < 1).astype(jnp.int32), jax.random.fold_in(key_of[4], 1), 0, 1)
    source_unit = draw_source_unit(jax.random.fold_in(key_of[6], 71), 0)
    return dict(queries=queries, keys=keys, values=values, gain=gain, starts=starts, source_unit=source_unit)


def reference(queries, keys, values, gain, starts, source_unit):
    offsets = jnp.arange(UNIT, dtype=jnp.int32)
    balanced_row = (source_unit.astype(jnp.int32)[:, None] * UNIT + offsets[None, :]).reshape(-1).astype(jnp.int32)
    q_feat = jax.nn.silu(queries[balanced_row].astype(jnp.float32)).astype(jnp.bfloat16)
    k_feat = jax.nn.silu(keys[balanced_row].astype(jnp.float32)).astype(jnp.bfloat16)
    v_bal = values[balanced_row]
    doc = jnp.cumsum(starts).astype(jnp.int32)
    block_count = TOKENS // BLK
    q_blocks = q_feat.reshape(block_count, BLK, HEADS, DH)
    k_blocks = k_feat.reshape(block_count, BLK, HEADS, DH)
    v_blocks = v_bal.reshape(block_count, BLK, HEADS, DH)
    doc_blocks = doc.reshape(block_count, BLK)
    causal = jnp.tril(jnp.ones((BLK, BLK), dtype=bool))

    def advance(carry, block):
        running, prior_doc = carry
        q_part, k_part, v_part, doc_part = block
        first_doc = doc_part[0]
        entering = jnp.where(first_doc == prior_doc, running, jnp.zeros_like(running)).astype(jnp.bfloat16)
        carried = jnp.einsum('thd,hde->the', q_part.astype(jnp.float32), entering.astype(jnp.float32))
        scores = jnp.einsum('thd,shd->hts', q_part.astype(jnp.float32), k_part.astype(jnp.float32))
        allowed = causal & (doc_part[:, None] == doc_part[None, :])
        weights = jnp.where(allowed[None], scores, jnp.zeros_like(scores)).astype(jnp.bfloat16)
        within = jnp.einsum('hts,she->the', weights.astype(jnp.float32), v_part.astype(jnp.float32))
        seen = (doc_part == first_doc)[:, None, None]
        attended = jnp.where(seen, carried, jnp.zeros_like(carried)) + within
        last_doc = doc_part[BLK - 1]
        recent = jnp.where((doc_part == last_doc)[:, None, None], k_part, jnp.zeros_like(k_part))
        block_state = jnp.einsum('shd,she->hde', recent.astype(jnp.float32), v_part.astype(jnp.float32))
        running = jnp.where(last_doc == prior_doc, running, jnp.zeros_like(running)) + block_state
        return ((running, last_doc), attended)
    initial = (jnp.zeros((HEADS, DH, DH), jnp.float32), jnp.array(-1, dtype=jnp.int32))
    _, attended = lax.scan(advance, initial, (q_blocks, k_blocks, v_blocks, doc_blocks))
    flat = attended.reshape(TOKENS, HEADS * DH)
    mean_square = lax.optimization_barrier(jnp.mean(flat * flat, axis=-1, keepdims=True))
    return (flat * lax.rsqrt(mean_square + 1e-06) * gain).astype(jnp.bfloat16)
```

```python
import functools
import jax
import jax.numpy as jnp
from jax import lax
from jax.experimental import pallas as pl
from jax.experimental.pallas import tpu as pltpu
from jax.sharding import PartitionSpec as P

DH = 128
CAP = 2
BLK = 768
TILE = 256
GROUPS = 4
WINDOW = 2
MESH = pl.DeviceIdType.MESH


def silu(x):
    x = x.astype(jnp.float32)
    return (x / (1.0 + jnp.exp(-x))).astype(jnp.bfloat16)


def exchange_kernel(
    n, tp, q_in, k_in, v_in, chosen, lookup, flags, doc_col, doc_row,
    out, sums, staged, packed, arrived, q_ord, k_ord, v_ord, chain_in, chain_out, block_state,
    out_buf, squares, own_sum, tp_in,
    stage_sem, send_sem, recv_sem, chain_send, chain_recv, out_sem, tp_send, tp_recv,
):
    me = lax.axis_index("ctx")
    my_tp = lax.axis_index("tp")
    slots, unit_rows, _ = q_in.shape
    group_heads = q_ord.shape[0]
    width = group_heads * DH
    tokens = slots * unit_rows
    blocks = tokens // BLK
    sources = []
    for g in range(GROUPS):
        sources += [(k_in, g, True), (v_in, g, False)]
    sources += [(q_in, g, True) for g in range(GROUPS)]
    pieces = len(sources)

    def stage(i):
        ref, g, _ = sources[i]
        return pltpu.make_async_copy(
            ref.at[:, :, pl.ds(g * width, width)], staged[i % 2], stage_sem.at[i % 2]
        )

    def prepare(i):
        stage(i).wait()
        feature = sources[i][2]

        def one(u, _):
            rows = staged[i % 2][chosen[u]]
            rows = silu(rows) if feature else rows
            for h in range(group_heads):
                packed[i, u, h] = rows[:, h * DH : (h + 1) * DH]
            return 0

        lax.fori_loop(0, slots, one, 0)
        if i + 2 < pieces:
            stage(i + 2).start()
        mine = pl.ds(CAP * me, CAP)
        arrived[i][mine] = packed[i, mine]

    def remote(i, off):
        to = lax.rem(me + off, n)
        return pltpu.make_async_remote_copy(
            src_ref=packed.at[i, pl.ds(CAP * to, CAP)],
            dst_ref=arrived[i].at[pl.ds(CAP * me, CAP)],
            send_sem=send_sem.at[i, off - 1],
            recv_sem=recv_sem.at[i, off - 1],
            device_id={"ctx": to},
            device_id_type=MESH,
        )

    def each_peer(i, action):
        def one(off, _):
            action(remote(i, off))
            return 0

        lax.fori_loop(1, n, one, 0)

    def unpack(i, target):
        def one(u, _):
            rows = pl.ds(pl.multiple_of(u * unit_rows, unit_rows), unit_rows)
            target[:, rows, :] = arrived[i][lookup[u]]
            return 0

        lax.fori_loop(0, slots, one, 0)

    def chain(g):
        return pltpu.make_async_remote_copy(
            src_ref=chain_out.at[g],
            dst_ref=chain_in.at[g],
            send_sem=chain_send.at[g],
            recv_sem=chain_recv.at[g],
            device_id={"ctx": lax.rem(me + 1, n)},
            device_id_type=MESH,
        )

    def states(g):
        each_peer(2 * g, lambda c: c.wait_recv())
        each_peer(2 * g + 1, lambda c: c.wait_recv())
        unpack(2 * g, k_ord)
        unpack(2 * g + 1, v_ord)
        for b in range(blocks):
            rows = slice(b * BLK, (b + 1) * BLK)
            last = doc_col[(b + 1) * BLK - 1 : (b + 1) * BLK, :]
            recent = doc_col[rows, :] == last

            def one(h, _):
                keys = jnp.where(recent, k_ord[h, rows, :], 0.0).astype(jnp.bfloat16)
                block_state[g, b, h] = lax.dot_general(
                    keys, v_ord[h, rows, :], (((0,), (0,)), ((), ())),
                    preferred_element_type=jnp.float32,
                )
                return 0

            lax.fori_loop(0, group_heads, one, 0)

        @pl.when(me == 0)
        def _():
            chain_in[g] = jnp.zeros_like(chain_in[g])

        @pl.when(me > 0)
        def _():
            chain(g).wait_recv()

        @pl.when(me < n - 1)
        def _():
            running = chain_in[g].astype(jnp.float32)
            for b in range(blocks):
                running = flags[0, b] * running + block_state[g, b]
            chain_out[g] = running.astype(jnp.bfloat16)
            chain(g).start()

    def out_copy(g):
        return pltpu.make_async_copy(
            out_buf.at[g % 2], out.at[:, pl.ds(g * width, width)], out_sem.at[g % 2]
        )

    def attend(g):
        each_peer(2 * GROUPS + g, lambda c: c.wait_recv())
        unpack(2 * GROUPS + g, q_ord)
        unpack(2 * g, k_ord)
        unpack(2 * g + 1, v_ord)
        if g >= 2:
            out_copy(g - 2).wait()
        for b in range(blocks):
            for t in range(BLK // TILE):
                first = b * BLK
                rows = slice(first + t * TILE, first + (t + 1) * TILE)
                keys = slice(first, first + (t + 1) * TILE)
                span = (t + 1) * TILE
                here = doc_col[rows, :]
                causal = lax.broadcasted_iota(jnp.int32, (TILE, span), 1) <= (
                    lax.broadcasted_iota(jnp.int32, (TILE, span), 0) + t * TILE
                )
                allowed = causal & (here[:, :1] == doc_row[:1, keys])
                seen = here == doc_col[first : first + 1, :]

                def one(h, _):
                    running = chain_in[g, h].astype(jnp.float32)
                    for p in range(b):
                        running = flags[0, p] * running + block_state[g, p, h]
                    entering = (flags[1, b] * running).astype(jnp.bfloat16)
                    query = q_ord[h, rows, :]
                    scores = lax.dot_general(
                        query, k_ord[h, keys, :], (((1,), (1,)), ((), ())),
                        preferred_element_type=jnp.float32,
                    )
                    weights = jnp.where(allowed, scores, 0.0).astype(jnp.bfloat16)
                    within = jnp.dot(
                        weights, v_ord[h, keys, :], preferred_element_type=jnp.float32
                    )
                    carried = jnp.dot(query, entering, preferred_element_type=jnp.float32)
                    total = within + jnp.where(seen, carried, 0.0)
                    squares[rows, :] += total * total
                    columns = pl.ds(pl.multiple_of(h * DH, DH), DH)
                    out_buf[g % 2, rows, columns] = total.astype(jnp.bfloat16)
                    return 0

                lax.fori_loop(0, group_heads, one, 0)
        out_copy(g).start()

    def tp_copy(off):
        return pltpu.make_async_remote_copy(
            src_ref=own_sum,
            dst_ref=tp_in.at[off - 1],
            send_sem=tp_send.at[off - 1],
            recv_sem=tp_recv.at[off - 1],
            device_id={"tp": lax.rem(my_tp + off, tp)},
            device_id_type=MESH,
        )

    barrier = pltpu.get_barrier_semaphore()
    stage(0).start()
    stage(1).start()

    def greet_ctx(off, _):
        pl.semaphore_signal(
            barrier, inc=1, device_id={"ctx": lax.rem(me + off, n)}, device_id_type=MESH
        )
        return 0

    def greet_tp(off, _):
        pl.semaphore_signal(
            barrier, inc=1, device_id={"tp": lax.rem(my_tp + off, tp)}, device_id_type=MESH
        )
        return 0

    lax.fori_loop(1, n, greet_ctx, 0)
    lax.fori_loop(1, tp, greet_tp, 0)
    prepare(0)
    pl.semaphore_wait(barrier, n - 1 + tp - 1)
    squares[...] = jnp.zeros_like(squares)

    for i in range(pieces):
        if i > 0:
            prepare(i)
        if i >= WINDOW:
            each_peer(i - WINDOW, lambda c: c.wait_send())
        each_peer(i, lambda c: c.start())
        done = i - WINDOW
        if 0 <= done < 2 * GROUPS and done % 2 == 1:
            states(done // 2)
        elif done >= 2 * GROUPS:
            attend(done - 2 * GROUPS)
    for i in range(pieces - WINDOW, pieces):
        attend(i - 2 * GROUPS)
    own_sum[...] = lax.dot_general(
        jnp.ones((8, DH), jnp.float32), squares[...], (((1,), (1,)), ((), ())),
        preferred_element_type=jnp.float32, precision=lax.Precision.HIGHEST,
    )
    for off in range(1, tp):
        tp_copy(off).start()
    for i in range(pieces - WINDOW, pieces):
        each_peer(i, lambda c: c.wait_send())

    @pl.when(me < n - 1)
    def _():
        for g in range(GROUPS):
            chain(g).wait_send()

    for g in range(max(GROUPS - 2, 0), GROUPS):
        out_copy(g).wait()
    total = own_sum[...]
    for off in range(1, tp):
        tp_copy(off).wait_recv()
        total = total + tp_in[off - 1]
    for off in range(1, tp):
        tp_copy(off).wait_send()
    sums[...] = total


def fused(queries, keys, values, gain, starts, source_unit):
    n = lax.axis_size("ctx")
    tp = lax.axis_size("tp")
    my_index = lax.axis_index("ctx")
    tokens, columns = queries.shape
    slots = CAP * n
    unit_rows = tokens // slots
    heads = columns // DH
    group_heads = heads // GROUPS
    blocks = tokens // BLK
    owners = source_unit.reshape(n, slots)
    source_shard = owners // slots
    source_slot = owners % slots
    earlier = jnp.arange(slots)[None, :] < jnp.arange(slots)[:, None]
    same_source = source_shard[:, :, None] == source_shard[:, None, :]
    rank = jnp.sum(jnp.where(same_source & earlier[None], 1, 0), axis=2).astype(jnp.int32)
    matches = (source_shard == my_index)[:, None, :] & (
        rank[:, None, :] == jnp.arange(CAP, dtype=jnp.int32)[None, :, None]
    )
    chosen = jnp.sum(jnp.where(matches, source_slot[:, None, :], 0), axis=2).reshape(-1)
    lookup = lax.dynamic_index_in_dim(source_shard * CAP + rank, my_index, 0, keepdims=False)
    doc = jnp.cumsum(starts).astype(jnp.int32)
    block_starts = starts.reshape(blocks, BLK)
    flags = jnp.stack(
        [jnp.where(jnp.any(block_starts > 0, axis=1), 0.0, 1.0),
         jnp.where(block_starts[:, 0] > 0, 0.0, 1.0)]
    ).astype(jnp.float32)
    doc_col = jnp.broadcast_to(doc[:, None], (tokens, DH))
    doc_row = jnp.broadcast_to(doc[None, :], (8, tokens))
    pieces = 3 * GROUPS
    piece = (slots, group_heads, unit_rows, DH)
    bf16, f32 = jnp.bfloat16, jnp.float32
    hbm = pl.BlockSpec(memory_space=pl.ANY)
    smem = pl.BlockSpec(memory_space=pltpu.SMEM)
    vmem = pl.BlockSpec(memory_space=pltpu.VMEM)
    ordered = pltpu.VMEM((group_heads, tokens, DH), bf16)
    dma = pltpu.SemaphoreType.DMA
    attended, sums = pl.pallas_call(
        functools.partial(exchange_kernel, n, tp),
        out_shape=(
            jax.ShapeDtypeStruct((tokens, columns), bf16),
            jax.ShapeDtypeStruct((8, tokens), f32),
        ),
        in_specs=[hbm, hbm, hbm, smem, smem, smem, vmem, vmem],
        out_specs=(hbm, vmem),
        scratch_shapes=[
            [pltpu.VMEM((slots, unit_rows, group_heads * DH), bf16) for _ in range(2)],
            pltpu.VMEM((pieces,) + piece, bf16),
            [pltpu.VMEM(piece, bf16) for _ in range(pieces)],
            ordered, ordered, ordered,
            pltpu.VMEM((GROUPS, group_heads, DH, DH), bf16),
            pltpu.VMEM((GROUPS, group_heads, DH, DH), bf16),
            pltpu.VMEM((GROUPS, blocks, group_heads, DH, DH), f32),
            pltpu.VMEM((2, tokens, group_heads * DH), bf16),
            pltpu.VMEM((tokens, DH), f32),
            pltpu.VMEM((8, tokens), f32),
            pltpu.VMEM((max(tp - 1, 1), 8, tokens), f32),
            dma((2,)),
            dma((pieces, n - 1)),
            dma((pieces, n - 1)),
            dma((GROUPS,)),
            dma((GROUPS,)),
            dma((2,)),
            dma((max(tp - 1, 1),)),
            dma((max(tp - 1, 1),)),
        ],
        compiler_params=pltpu.CompilerParams(
            collective_id=0, has_side_effects=True, vmem_limit_bytes=62 * 1024 * 1024
        ),
    )(
        queries.reshape(slots, unit_rows, columns),
        keys.reshape(slots, unit_rows, columns),
        values.reshape(slots, unit_rows, columns),
        chosen, lookup, flags, doc_col, doc_row,
    )
    mean_square = sums[0] / (columns * tp)
    scale = lax.rsqrt(mean_square + 1e-06)[:, None]
    return (attended.astype(f32) * scale * gain).astype(bf16)


def local(queries, keys, values, gain, starts, source_unit):
    shard_count = lax.axis_size("ctx")
    my_index = lax.axis_index("ctx")
    token_count, column_count = queries.shape
    slot_count = 2 * shard_count
    unit_rows = token_count // slot_count
    head_count = column_count // DH
    owners = source_unit.reshape(shard_count, slot_count)
    source_shard = owners // slot_count
    source_slot = owners % slot_count
    earlier_slot = jnp.arange(slot_count)[None, :] < jnp.arange(slot_count)[:, None]
    same_source = source_shard[:, :, None] == source_shard[:, None, :]
    arrival_rank = jnp.sum(jnp.where(same_source & earlier_slot[None], 1, 0), axis=2).astype(
        jnp.int32
    )
    from_me = source_shard == my_index
    matches = from_me[:, None, :] & (
        arrival_rank[:, None, :] == jnp.arange(CAP, dtype=jnp.int32)[None, :, None]
    )
    chosen = jnp.sum(jnp.where(matches, source_slot[:, None, :], 0), axis=2).reshape(-1)
    occupied = jnp.any(matches, axis=2).reshape(-1)

    def packed(array):
        pieces = array.reshape(slot_count, unit_rows, column_count)[chosen]
        pieces = jnp.where(occupied[:, None, None], pieces, jnp.zeros_like(pieces))
        return pieces.reshape(shard_count, CAP * unit_rows, column_count)

    arrived = (
        lax.all_to_all(packed(queries), "ctx", split_axis=0, concat_axis=0, tiled=True),
        lax.all_to_all(packed(keys), "ctx", split_axis=0, concat_axis=0, tiled=True),
        lax.all_to_all(packed(values), "ctx", split_axis=0, concat_axis=0, tiled=True),
    )
    my_source = lax.dynamic_index_in_dim(source_shard, my_index, 0, keepdims=False)
    my_rank = lax.dynamic_index_in_dim(arrival_rank, my_index, 0, keepdims=False)
    lookup = my_source * CAP + my_rank

    def unpacked(array):
        return array.reshape(shard_count * CAP, unit_rows, column_count)[lookup].reshape(
            token_count, column_count
        )

    block_count = token_count // BLK
    q_feat = (
        jax.nn.silu(unpacked(arrived[0]).astype(jnp.float32))
        .astype(jnp.bfloat16)
        .reshape(block_count, BLK, head_count, DH)
    )
    k_feat = (
        jax.nn.silu(unpacked(arrived[1]).astype(jnp.float32))
        .astype(jnp.bfloat16)
        .reshape(block_count, BLK, head_count, DH)
    )
    v_bal = unpacked(arrived[2]).reshape(block_count, BLK, head_count, DH)
    block_starts = starts.reshape(block_count, BLK)
    local_doc = jnp.cumsum(starts).reshape(block_count, BLK)
    last_doc = local_doc[:, BLK - 1 :]
    recent = jnp.where((local_doc == last_doc)[:, :, None, None], k_feat, jnp.zeros_like(k_feat))
    block_states = jnp.einsum("bshd,bshe->bhde", recent, v_bal, preferred_element_type=jnp.float32)
    has_start = jnp.any(block_starts > 0, axis=1)
    opening = block_starts[:, 0] > 0
    running = jnp.zeros((head_count, DH, DH), jnp.float32)
    for position in range(block_count):
        running = jnp.where(has_start[position], 0.0, running) + block_states[position]
    shard_flag = jnp.any(starts > 0).astype(jnp.float32).reshape(1)
    all_flags = lax.all_gather(shard_flag, "ctx", axis=0, tiled=True)
    shard_ids = jnp.arange(shard_count, dtype=jnp.int32)
    lowest = jnp.max(jnp.where((shard_ids < my_index) & (all_flags > 0), shard_ids, 0))
    piece = lax.all_gather(running[None], "ctx", axis=0, tiled=True)
    ids = jnp.arange(piece.shape[0], dtype=jnp.int32)
    wanted = (ids >= lowest) & (ids < my_index)
    incoming = jnp.sum(jnp.where(wanted[:, None, None, None], piece, 0.0), axis=0)
    causal = jnp.tril(jnp.ones((BLK, BLK), dtype=bool))
    scores = jnp.einsum("bthd,bshd->bhts", q_feat, k_feat, preferred_element_type=jnp.float32)
    allowed = causal[None] & (local_doc[:, :, None] == local_doc[:, None, :])
    weights = jnp.where(allowed[:, None], scores, 0.0).astype(jnp.bfloat16)
    within = jnp.einsum("bhts,bshe->bthe", weights, v_bal, preferred_element_type=jnp.float32)
    carry_state = incoming
    carried_parts = []
    for position in range(block_count):
        entering = jnp.where(opening[position], 0.0, carry_state).astype(jnp.bfloat16)
        carried = jnp.einsum(
            "thd,hde->the", q_feat[position], entering, preferred_element_type=jnp.float32
        )
        seen = local_doc[position] == local_doc[position, 0]
        carried_parts.append(jnp.where(seen[:, None, None], carried, 0.0))
        carry_state = jnp.where(has_start[position], 0.0, carry_state) + block_states[position]
    attended = jnp.stack(carried_parts) + within
    flat = attended.reshape(token_count, column_count)
    square_sums = lax.psum(jnp.sum(flat * flat, axis=1), "tp")
    mean_square = square_sums / (column_count * lax.axis_size("tp"))
    return (flat * lax.rsqrt(mean_square + 1e-06)[:, None] * gain).astype(jnp.bfloat16)


def solution(mesh):
    in_specs = (P("ctx", "tp"), P("ctx", "tp"), P("ctx", "tp"), P("tp"), P("ctx"), P())
    out_specs = P("ctx", "tp")

    def body(queries, keys, values, gain, starts, source_unit):
        unit_rows = queries.shape[0] // (CAP * mesh.shape["ctx"])
        whole = unit_rows % 16 == 0 and queries.shape[1] % (GROUPS * DH) == 0
        return (fused if whole else local)(queries, keys, values, gain, starts, source_unit)

    return jax.shard_map(body, mesh=mesh, in_specs=in_specs, out_specs=out_specs, check_vma=False)
```

```python
import functools
import jax
import jax.numpy as jnp
from jax import lax
from jax.experimental import pallas as pl
from jax.experimental.pallas import tpu as pltpu
from jax.sharding import PartitionSpec as P

DH = 128
CAP = 2
BLK = 768
TILE = 256
GROUPS = 8
WINDOW = 4
STAGGER = 5
MESH = pl.DeviceIdType.MESH


def silu(x):
    x = x.astype(jnp.float32)
    return (x / (1.0 + jnp.exp(-x))).astype(jnp.bfloat16)


def exchange_kernel(
    n, tp, q_in, k_in, v_in, chosen, lookup, flags, doc_col, doc_row,
    out, sums, staged, packed, arrived, q_ord, k_ord, v_ord, chain_in, chain_out, block_state,
    out_buf, squares, own_sum, tp_in,
    stage_sem, send_sem, recv_sem, chain_send, chain_recv, out_sem, tp_send, tp_recv,
):
    me = lax.axis_index("ctx")
    my_tp = lax.axis_index("tp")
    slots, unit_rows, _ = q_in.shape
    group_heads = q_ord.shape[0]
    width = group_heads * DH
    tokens = slots * unit_rows
    blocks = tokens // BLK
    sources = []
    for g in range(GROUPS):
        sources += [(k_in, g, True), (v_in, g, False)]
    sources += [(q_in, g, True) for g in range(GROUPS)]
    pieces = len(sources)

    def stage(i):
        ref, g, _ = sources[i]
        return pltpu.make_async_copy(
            ref.at[:, :, pl.ds(g * width, width)], staged[i % 2], stage_sem.at[i % 2]
        )

    def prepare(i):
        stage(i).wait()
        feature = sources[i][2]

        def one(u, _):
            rows = staged[i % 2][chosen[u]]
            rows = silu(rows) if feature else rows
            for h in range(group_heads):
                packed[i, u, h] = rows[:, h * DH : (h + 1) * DH]
            return 0

        lax.fori_loop(0, slots, one, 0)
        if i + 2 < pieces:
            stage(i + 2).start()
        mine = pl.ds(CAP * me, CAP)
        arrived[i][mine] = packed[i, mine]

    half = n // 2
    side, place = me // half, lax.rem(me, half)

    def remote(i, off):
        turn = lax.rem(off - 1 + lax.rem(my_tp, 2), n - 1)
        other = 1 - lax.rem(turn, 2)
        step = (turn + 1) // 2
        to = lax.rem(side + other, 2) * half + lax.rem(place + step, half)
        return pltpu.make_async_remote_copy(
            src_ref=packed.at[i, pl.ds(CAP * to, CAP)],
            dst_ref=arrived[i].at[pl.ds(CAP * me, CAP)],
            send_sem=send_sem.at[i, turn],
            recv_sem=recv_sem.at[i, turn],
            device_id={"ctx": to},
            device_id_type=MESH,
        )

    def each_peer(i, action):
        def one(off, _):
            action(remote(i, off))
            return 0

        lax.fori_loop(1, n, one, 0)

    def unpack(i, target):
        def one(u, _):
            rows = pl.ds(pl.multiple_of(u * unit_rows, unit_rows), unit_rows)
            target[:, rows, :] = arrived[i][lookup[u]]
            return 0

        lax.fori_loop(0, slots, one, 0)

    def chain(g):
        return pltpu.make_async_remote_copy(
            src_ref=chain_out.at[g],
            dst_ref=chain_in.at[g],
            send_sem=chain_send.at[g],
            recv_sem=chain_recv.at[g],
            device_id={"ctx": lax.rem(me + 1, n)},
            device_id_type=MESH,
        )

    def states(g):
        each_peer(2 * g, lambda c: c.wait_recv())
        each_peer(2 * g + 1, lambda c: c.wait_recv())
        unpack(2 * g, k_ord)
        unpack(2 * g + 1, v_ord)
        for b in range(blocks):
            rows = slice(b * BLK, (b + 1) * BLK)
            last = doc_col[(b + 1) * BLK - 1 : (b + 1) * BLK, :]
            recent = doc_col[rows, :] == last

            def one(h, _):
                keys = jnp.where(recent, k_ord[h, rows, :], 0.0).astype(jnp.bfloat16)
                block_state[g, b, h] = lax.dot_general(
                    keys, v_ord[h, rows, :], (((0,), (0,)), ((), ())),
                    preferred_element_type=jnp.float32,
                )
                return 0

            lax.fori_loop(0, group_heads, one, 0)

    def pass_on(g):
        @pl.when(me > 0)
        def _():
            chain(g).wait_recv()

        @pl.when(me < n - 1)
        def _():
            running = chain_in[g].astype(jnp.float32)
            for b in range(blocks):
                running = flags[0, b] * running + block_state[g, b]
            chain_out[g] = running.astype(jnp.bfloat16)
            chain(g).start()

    def out_copy(g):
        return pltpu.make_async_copy(
            out_buf.at[g % 2], out.at[:, pl.ds(g * width, width)], out_sem.at[g % 2]
        )

    def attend(g):
        each_peer(2 * GROUPS + g, lambda c: c.wait_recv())
        unpack(2 * GROUPS + g, q_ord)
        unpack(2 * g, k_ord)
        unpack(2 * g + 1, v_ord)
        if g >= 2:
            out_copy(g - 2).wait()
        for b in range(blocks):
            for t in range(BLK // TILE):
                first = b * BLK
                rows = slice(first + t * TILE, first + (t + 1) * TILE)
                keys = slice(first, first + (t + 1) * TILE)
                span = (t + 1) * TILE
                here = doc_col[rows, :]
                causal = lax.broadcasted_iota(jnp.int32, (TILE, span), 1) <= (
                    lax.broadcasted_iota(jnp.int32, (TILE, span), 0) + t * TILE
                )
                allowed = causal & (here[:, :1] == doc_row[:1, keys])
                seen = here == doc_col[first : first + 1, :]

                def one(h, _):
                    running = chain_in[g, h].astype(jnp.float32)
                    for p in range(b):
                        running = flags[0, p] * running + block_state[g, p, h]
                    entering = (flags[1, b] * running).astype(jnp.bfloat16)
                    query = q_ord[h, rows, :]
                    scores = lax.dot_general(
                        query, k_ord[h, keys, :], (((1,), (1,)), ((), ())),
                        preferred_element_type=jnp.float32,
                    )
                    weights = jnp.where(allowed, scores, 0.0).astype(jnp.bfloat16)
                    within = jnp.dot(
                        weights, v_ord[h, keys, :], preferred_element_type=jnp.float32
                    )
                    carried = jnp.dot(query, entering, preferred_element_type=jnp.float32)
                    total = within + jnp.where(seen, carried, 0.0)
                    squares[rows, :] += total * total
                    columns = pl.ds(pl.multiple_of(h * DH, DH), DH)
                    out_buf[g % 2, rows, columns] = total.astype(jnp.bfloat16)
                    return 0

                lax.fori_loop(0, group_heads, one, 0)
        out_copy(g).start()

    def tp_copy(off):
        return pltpu.make_async_remote_copy(
            src_ref=own_sum,
            dst_ref=tp_in.at[off - 1],
            send_sem=tp_send.at[off - 1],
            recv_sem=tp_recv.at[off - 1],
            device_id={"tp": lax.rem(my_tp + off, tp)},
            device_id_type=MESH,
        )

    def follow(done):
        if 0 <= done < 2 * GROUPS and done % 2 == 1:
            states(done // 2)
        if 1 <= done < 2 * GROUPS + STAGGER:
            late = done - 1 - me * STAGGER // n

            @pl.when((late >= 0) & (lax.rem(late, 2) == 0) & (late < 2 * GROUPS))
            def _():
                pass_on(late // 2)

        if done >= 2 * GROUPS:
            attend(done - 2 * GROUPS)

    barrier = pltpu.get_barrier_semaphore()
    stage(0).start()
    stage(1).start()

    def greet_ctx(off, _):
        pl.semaphore_signal(
            barrier, inc=1, device_id={"ctx": lax.rem(me + off, n)}, device_id_type=MESH
        )
        return 0

    def greet_tp(off, _):
        pl.semaphore_signal(
            barrier, inc=1, device_id={"tp": lax.rem(my_tp + off, tp)}, device_id_type=MESH
        )
        return 0

    lax.fori_loop(1, n, greet_ctx, 0)
    lax.fori_loop(1, tp, greet_tp, 0)
    prepare(0)
    pl.semaphore_wait(barrier, n - 1 + tp - 1)
    squares[...] = jnp.zeros_like(squares)

    @pl.when(me == 0)
    def _():
        chain_in[...] = jnp.zeros_like(chain_in)


    for i in range(pieces):
        if i > 0:
            prepare(i)
        if i >= WINDOW:
            each_peer(i - WINDOW, lambda c: c.wait_send())
        each_peer(i, lambda c: c.start())
        follow(i - WINDOW)
    for i in range(pieces - WINDOW, pieces):
        follow(i)
    own_sum[...] = lax.dot_general(
        jnp.ones((8, DH), jnp.float32), squares[...], (((1,), (1,)), ((), ())),
        preferred_element_type=jnp.float32, precision=lax.Precision.HIGHEST,
    )
    for off in range(1, tp):
        tp_copy(off).start()
    for i in range(pieces - WINDOW, pieces):
        each_peer(i, lambda c: c.wait_send())

    @pl.when(me < n - 1)
    def _():
        for g in range(GROUPS):
            chain(g).wait_send()

    for g in range(max(GROUPS - 2, 0), GROUPS):
        out_copy(g).wait()
    total = own_sum[...]
    for off in range(1, tp):
        tp_copy(off).wait_recv()
        total = total + tp_in[off - 1]
    for off in range(1, tp):
        tp_copy(off).wait_send()
    sums[...] = total


def fused(queries, keys, values, gain, starts, source_unit):
    n = lax.axis_size("ctx")
    tp = lax.axis_size("tp")
    my_index = lax.axis_index("ctx")
    tokens, columns = queries.shape
    slots = CAP * n
    unit_rows = tokens // slots
    heads = columns // DH
    group_heads = heads // GROUPS
    blocks = tokens // BLK
    owners = source_unit.reshape(n, slots)
    source_shard = owners // slots
    source_slot = owners % slots
    earlier = jnp.arange(slots)[None, :] < jnp.arange(slots)[:, None]
    same_source = source_shard[:, :, None] == source_shard[:, None, :]
    rank = jnp.sum(jnp.where(same_source & earlier[None], 1, 0), axis=2).astype(jnp.int32)
    matches = (source_shard == my_index)[:, None, :] & (
        rank[:, None, :] == jnp.arange(CAP, dtype=jnp.int32)[None, :, None]
    )
    chosen = jnp.sum(jnp.where(matches, source_slot[:, None, :], 0), axis=2).reshape(-1)
    lookup = lax.dynamic_index_in_dim(source_shard * CAP + rank, my_index, 0, keepdims=False)
    doc = jnp.cumsum(starts).astype(jnp.int32)
    block_starts = starts.reshape(blocks, BLK)
    flags = jnp.stack(
        [jnp.where(jnp.any(block_starts > 0, axis=1), 0.0, 1.0),
         jnp.where(block_starts[:, 0] > 0, 0.0, 1.0)]
    ).astype(jnp.float32)
    doc_col = jnp.broadcast_to(doc[:, None], (tokens, DH))
    doc_row = jnp.broadcast_to(doc[None, :], (8, tokens))
    pieces = 3 * GROUPS
    piece = (slots, group_heads, unit_rows, DH)
    bf16, f32 = jnp.bfloat16, jnp.float32
    hbm = pl.BlockSpec(memory_space=pl.ANY)
    smem = pl.BlockSpec(memory_space=pltpu.SMEM)
    vmem = pl.BlockSpec(memory_space=pltpu.VMEM)
    ordered = pltpu.VMEM((group_heads, tokens, DH), bf16)
    dma = pltpu.SemaphoreType.DMA
    attended, sums = pl.pallas_call(
        functools.partial(exchange_kernel, n, tp),
        out_shape=(
            jax.ShapeDtypeStruct((tokens, columns), bf16),
            jax.ShapeDtypeStruct((8, tokens), f32),
        ),
        in_specs=[hbm, hbm, hbm, smem, smem, smem, vmem, vmem],
        out_specs=(hbm, vmem),
        scratch_shapes=[
            [pltpu.VMEM((slots, unit_rows, group_heads * DH), bf16) for _ in range(2)],
            pltpu.VMEM((pieces,) + piece, bf16),
            [pltpu.VMEM(piece, bf16) for _ in range(pieces)],
            ordered, ordered, ordered,
            pltpu.VMEM((GROUPS, group_heads, DH, DH), bf16),
            pltpu.VMEM((GROUPS, group_heads, DH, DH), bf16),
            pltpu.VMEM((GROUPS, blocks, group_heads, DH, DH), f32),
            pltpu.VMEM((2, tokens, group_heads * DH), bf16),
            pltpu.VMEM((tokens, DH), f32),
            pltpu.VMEM((8, tokens), f32),
            pltpu.VMEM((max(tp - 1, 1), 8, tokens), f32),
            dma((2,)),
            dma((pieces, n - 1)),
            dma((pieces, n - 1)),
            dma((GROUPS,)),
            dma((GROUPS,)),
            dma((2,)),
            dma((max(tp - 1, 1),)),
            dma((max(tp - 1, 1),)),
        ],
        compiler_params=pltpu.CompilerParams(
            collective_id=0, has_side_effects=True, vmem_limit_bytes=62 * 1024 * 1024
        ),
    )(
        queries.reshape(slots, unit_rows, columns),
        keys.reshape(slots, unit_rows, columns),
        values.reshape(slots, unit_rows, columns),
        chosen, lookup, flags, doc_col, doc_row,
    )
    mean_square = sums[0] / (columns * tp)
    scale = lax.rsqrt(mean_square + 1e-06)[:, None]
    return (attended.astype(f32) * scale * gain).astype(bf16)


def local(queries, keys, values, gain, starts, source_unit):
    shard_count = lax.axis_size("ctx")
    my_index = lax.axis_index("ctx")
    token_count, column_count = queries.shape
    slot_count = 2 * shard_count
    unit_rows = token_count // slot_count
    head_count = column_count // DH
    owners = source_unit.reshape(shard_count, slot_count)
    source_shard = owners // slot_count
    source_slot = owners % slot_count
    earlier_slot = jnp.arange(slot_count)[None, :] < jnp.arange(slot_count)[:, None]
    same_source = source_shard[:, :, None] == source_shard[:, None, :]
    arrival_rank = jnp.sum(jnp.where(same_source & earlier_slot[None], 1, 0), axis=2).astype(
        jnp.int32
    )
    from_me = source_shard == my_index
    matches = from_me[:, None, :] & (
        arrival_rank[:, None, :] == jnp.arange(CAP, dtype=jnp.int32)[None, :, None]
    )
    chosen = jnp.sum(jnp.where(matches, source_slot[:, None, :], 0), axis=2).reshape(-1)
    occupied = jnp.any(matches, axis=2).reshape(-1)

    def packed(array):
        pieces = array.reshape(slot_count, unit_rows, column_count)[chosen]
        pieces = jnp.where(occupied[:, None, None], pieces, jnp.zeros_like(pieces))
        return pieces.reshape(shard_count, CAP * unit_rows, column_count)

    arrived = (
        lax.all_to_all(packed(queries), "ctx", split_axis=0, concat_axis=0, tiled=True),
        lax.all_to_all(packed(keys), "ctx", split_axis=0, concat_axis=0, tiled=True),
        lax.all_to_all(packed(values), "ctx", split_axis=0, concat_axis=0, tiled=True),
    )
    my_source = lax.dynamic_index_in_dim(source_shard, my_index, 0, keepdims=False)
    my_rank = lax.dynamic_index_in_dim(arrival_rank, my_index, 0, keepdims=False)
    lookup = my_source * CAP + my_rank

    def unpacked(array):
        return array.reshape(shard_count * CAP, unit_rows, column_count)[lookup].reshape(
            token_count, column_count
        )

    block_count = token_count // BLK
    q_feat = (
        jax.nn.silu(unpacked(arrived[0]).astype(jnp.float32))
        .astype(jnp.bfloat16)
        .reshape(block_count, BLK, head_count, DH)
    )
    k_feat = (
        jax.nn.silu(unpacked(arrived[1]).astype(jnp.float32))
        .astype(jnp.bfloat16)
        .reshape(block_count, BLK, head_count, DH)
    )
    v_bal = unpacked(arrived[2]).reshape(block_count, BLK, head_count, DH)
    block_starts = starts.reshape(block_count, BLK)
    local_doc = jnp.cumsum(starts).reshape(block_count, BLK)
    last_doc = local_doc[:, BLK - 1 :]
    recent = jnp.where((local_doc == last_doc)[:, :, None, None], k_feat, jnp.zeros_like(k_feat))
    block_states = jnp.einsum("bshd,bshe->bhde", recent, v_bal, preferred_element_type=jnp.float32)
    has_start = jnp.any(block_starts > 0, axis=1)
    opening = block_starts[:, 0] > 0
    running = jnp.zeros((head_count, DH, DH), jnp.float32)
    for position in range(block_count):
        running = jnp.where(has_start[position], 0.0, running) + block_states[position]
    shard_flag = jnp.any(starts > 0).astype(jnp.float32).reshape(1)
    all_flags = lax.all_gather(shard_flag, "ctx", axis=0, tiled=True)
    shard_ids = jnp.arange(shard_count, dtype=jnp.int32)
    lowest = jnp.max(jnp.where((shard_ids < my_index) & (all_flags > 0), shard_ids, 0))
    piece = lax.all_gather(running[None], "ctx", axis=0, tiled=True)
    ids = jnp.arange(piece.shape[0], dtype=jnp.int32)
    wanted = (ids >= lowest) & (ids < my_index)
    incoming = jnp.sum(jnp.where(wanted[:, None, None, None], piece, 0.0), axis=0)
    causal = jnp.tril(jnp.ones((BLK, BLK), dtype=bool))
    scores = jnp.einsum("bthd,bshd->bhts", q_feat, k_feat, preferred_element_type=jnp.float32)
    allowed = causal[None] & (local_doc[:, :, None] == local_doc[:, None, :])
    weights = jnp.where(allowed[:, None], scores, 0.0).astype(jnp.bfloat16)
    within = jnp.einsum("bhts,bshe->bthe", weights, v_bal, preferred_element_type=jnp.float32)
    carry_state = incoming
    carried_parts = []
    for position in range(block_count):
        entering = jnp.where(opening[position], 0.0, carry_state).astype(jnp.bfloat16)
        carried = jnp.einsum(
            "thd,hde->the", q_feat[position], entering, preferred_element_type=jnp.float32
        )
        seen = local_doc[position] == local_doc[position, 0]
        carried_parts.append(jnp.where(seen[:, None, None], carried, 0.0))
        carry_state = jnp.where(has_start[position], 0.0, carry_state) + block_states[position]
    attended = jnp.stack(carried_parts) + within
    flat = attended.reshape(token_count, column_count)
    square_sums = lax.psum(jnp.sum(flat * flat, axis=1), "tp")
    mean_square = square_sums / (column_count * lax.axis_size("tp"))
    return (flat * lax.rsqrt(mean_square + 1e-06)[:, None] * gain).astype(jnp.bfloat16)


def solution(mesh):
    in_specs = (P("ctx", "tp"), P("ctx", "tp"), P("ctx", "tp"), P("tp"), P("ctx"), P())
    out_specs = P("ctx", "tp")

    def body(queries, keys, values, gain, starts, source_unit):
        unit_rows = queries.shape[0] // (CAP * mesh.shape["ctx"])
        whole = unit_rows % 16 == 0 and queries.shape[1] % (GROUPS * DH) == 0
        return (fused if whole else local)(queries, keys, values, gain, starts, source_unit)

    return jax.shard_map(body, mesh=mesh, in_specs=in_specs, out_specs=out_specs, check_vma=False)
```

```python
import functools
import jax
import jax.numpy as jnp
from jax import lax
from jax.experimental import pallas as pl
from jax.experimental.pallas import tpu as pltpu
from jax.sharding import PartitionSpec as P

DH = 128
CAP = 2
BLK = 768
TILE = 256
GROUPS = 8
WINDOW = 6
STAGGER = 8
MESH = pl.DeviceIdType.MESH


def silu(x):
    x = x.astype(jnp.float32)
    return (x / (1.0 + jnp.exp(-x))).astype(jnp.bfloat16)


def exchange_kernel(
    n, tp, q_in, k_in, v_in, chosen, lookup, flags, doc_col, doc_row,
    out, sums, staged, packed, arrived, q_ord, k_ord, v_ord, chain_in, chain_out, block_state,
    out_buf, squares, own_sum, tp_in,
    stage_sem, send_sem, recv_sem, chain_send, chain_recv, out_sem, tp_send, tp_recv,
):
    me = lax.axis_index("ctx")
    my_tp = lax.axis_index("tp")
    slots, unit_rows, _ = q_in.shape
    group_heads = q_ord.shape[0]
    width = group_heads * DH
    tokens = slots * unit_rows
    blocks = tokens // BLK
    sources = []
    for g in range(GROUPS):
        sources += [(k_in, g, True), (v_in, g, False)]
    sources += [(q_in, g, True) for g in range(GROUPS)]
    pieces = len(sources)

    def stage(i):
        ref, g, _ = sources[i]
        return pltpu.make_async_copy(
            ref.at[:, :, pl.ds(g * width, width)], staged[i % 2], stage_sem.at[i % 2]
        )

    def prepare(i):
        stage(i).wait()
        feature = sources[i][2]

        def one(u, _):
            rows = staged[i % 2][chosen[u]]
            rows = silu(rows) if feature else rows
            for h in range(group_heads):
                packed[i, u, h] = rows[:, h * DH : (h + 1) * DH]
            return 0

        lax.fori_loop(0, slots, one, 0)
        if i + 2 < pieces:
            stage(i + 2).start()
        mine = pl.ds(CAP * me, CAP)
        arrived[i][mine] = packed[i, mine]

    half = n // 2
    side, place = me // half, lax.rem(me, half)

    def remote(i, off):
        turn = lax.rem(off - 1 + lax.rem(my_tp, 2), n - 1)
        other = 1 - lax.rem(turn, 2)
        step = (turn + 1) // 2
        to = lax.rem(side + other, 2) * half + lax.rem(place + step, half)
        return pltpu.make_async_remote_copy(
            src_ref=packed.at[i, pl.ds(CAP * to, CAP)],
            dst_ref=arrived[i].at[pl.ds(CAP * me, CAP)],
            send_sem=send_sem.at[i, turn],
            recv_sem=recv_sem.at[i, turn],
            device_id={"ctx": to},
            device_id_type=MESH,
        )

    def each_peer(i, action):
        def one(off, _):
            action(remote(i, off))
            return 0

        lax.fori_loop(1, n, one, 0)

    def unpack(i, target):
        def one(u, _):
            rows = pl.ds(pl.multiple_of(u * unit_rows, unit_rows), unit_rows)
            target[:, rows, :] = arrived[i][lookup[u]]
            return 0

        lax.fori_loop(0, slots, one, 0)

    def chain(g):
        return pltpu.make_async_remote_copy(
            src_ref=chain_out.at[g],
            dst_ref=chain_in.at[g],
            send_sem=chain_send.at[g],
            recv_sem=chain_recv.at[g],
            device_id={"ctx": lax.rem(me + 1, n)},
            device_id_type=MESH,
        )

    def states(g):
        each_peer(2 * g, lambda c: c.wait_recv())
        each_peer(2 * g + 1, lambda c: c.wait_recv())
        unpack(2 * g, k_ord)
        unpack(2 * g + 1, v_ord)
        for b in range(blocks):
            rows = slice(b * BLK, (b + 1) * BLK)
            last = doc_col[(b + 1) * BLK - 1 : (b + 1) * BLK, :]
            recent = doc_col[rows, :] == last

            def one(h, _):
                keys = jnp.where(recent, k_ord[h, rows, :], 0.0).astype(jnp.bfloat16)
                block_state[g, b, h] = lax.dot_general(
                    keys, v_ord[h, rows, :], (((0,), (0,)), ((), ())),
                    preferred_element_type=jnp.float32,
                )
                return 0

            lax.fori_loop(0, group_heads, one, 0)

    def pass_on(g):
        @pl.when(me > 0)
        def _():
            chain(g).wait_recv()

        @pl.when(me < n - 1)
        def _():
            running = chain_in[g].astype(jnp.float32)
            for b in range(blocks):
                running = flags[0, b] * running + block_state[g, b]
            chain_out[g] = running.astype(jnp.bfloat16)
            chain(g).start()

    def out_copy(g):
        return pltpu.make_async_copy(
            out_buf.at[g % 2], out.at[:, pl.ds(g * width, width)], out_sem.at[g % 2]
        )

    def attend(g):
        each_peer(2 * GROUPS + g, lambda c: c.wait_recv())
        unpack(2 * GROUPS + g, q_ord)
        unpack(2 * g, k_ord)
        unpack(2 * g + 1, v_ord)
        if g >= 2:
            out_copy(g - 2).wait()
        for b in range(blocks):
            for t in range(BLK // TILE):
                first = b * BLK
                rows = slice(first + t * TILE, first + (t + 1) * TILE)
                keys = slice(first, first + (t + 1) * TILE)
                span = (t + 1) * TILE
                here = doc_col[rows, :]
                causal = lax.broadcasted_iota(jnp.int32, (TILE, span), 1) <= (
                    lax.broadcasted_iota(jnp.int32, (TILE, span), 0) + t * TILE
                )
                allowed = causal & (here[:, :1] == doc_row[:1, keys])
                seen = here == doc_col[first : first + 1, :]

                def one(h, _):
                    running = chain_in[g, h].astype(jnp.float32)
                    for p in range(b):
                        running = flags[0, p] * running + block_state[g, p, h]
                    entering = (flags[1, b] * running).astype(jnp.bfloat16)
                    query = q_ord[h, rows, :]
                    scores = lax.dot_general(
                        query, k_ord[h, keys, :], (((1,), (1,)), ((), ())),
                        preferred_element_type=jnp.float32,
                    )
                    weights = jnp.where(allowed, scores, 0.0).astype(jnp.bfloat16)
                    within = jnp.dot(
                        weights, v_ord[h, keys, :], preferred_element_type=jnp.float32
                    )
                    carried = jnp.dot(query, entering, preferred_element_type=jnp.float32)
                    total = within + jnp.where(seen, carried, 0.0)
                    squares[rows, :] += total * total
                    columns = pl.ds(pl.multiple_of(h * DH, DH), DH)
                    out_buf[g % 2, rows, columns] = total.astype(jnp.bfloat16)
                    return 0

                lax.fori_loop(0, group_heads, one, 0)
        out_copy(g).start()

    def tp_copy(off):
        return pltpu.make_async_remote_copy(
            src_ref=own_sum,
            dst_ref=tp_in.at[off - 1],
            send_sem=tp_send.at[off - 1],
            recv_sem=tp_recv.at[off - 1],
            device_id={"tp": lax.rem(my_tp + off, tp)},
            device_id_type=MESH,
        )

    def follow(done):
        if 0 <= done < 2 * GROUPS and done % 2 == 1:
            states(done // 2)
        if 1 <= done < 2 * GROUPS + STAGGER:
            late = done - 1 - me * STAGGER // n

            @pl.when((late >= 0) & (lax.rem(late, 2) == 0) & (late < 2 * GROUPS))
            def _():
                pass_on(late // 2)

        if done >= 2 * GROUPS:
            attend(done - 2 * GROUPS)

    barrier = pltpu.get_barrier_semaphore()
    stage(0).start()
    stage(1).start()

    def greet_ctx(off, _):
        pl.semaphore_signal(
            barrier, inc=1, device_id={"ctx": lax.rem(me + off, n)}, device_id_type=MESH
        )
        return 0

    def greet_tp(off, _):
        pl.semaphore_signal(
            barrier, inc=1, device_id={"tp": lax.rem(my_tp + off, tp)}, device_id_type=MESH
        )
        return 0

    lax.fori_loop(1, n, greet_ctx, 0)
    lax.fori_loop(1, tp, greet_tp, 0)
    prepare(0)
    pl.semaphore_wait(barrier, n - 1 + tp - 1)
    squares[...] = jnp.zeros_like(squares)

    @pl.when(me == 0)
    def _():
        chain_in[...] = jnp.zeros_like(chain_in)


    for i in range(pieces):
        if i > 0:
            prepare(i)
        if i >= WINDOW:
            each_peer(i - WINDOW, lambda c: c.wait_send())
        each_peer(i, lambda c: c.start())
        follow(i - WINDOW)
    for i in range(pieces - WINDOW, pieces):
        follow(i)
    own_sum[...] = lax.dot_general(
        jnp.ones((8, DH), jnp.float32), squares[...], (((1,), (1,)), ((), ())),
        preferred_element_type=jnp.float32, precision=lax.Precision.HIGHEST,
    )
    for off in range(1, tp):
        tp_copy(off).start()
    for i in range(pieces - WINDOW, pieces):
        each_peer(i, lambda c: c.wait_send())

    @pl.when(me < n - 1)
    def _():
        for g in range(GROUPS):
            chain(g).wait_send()

    for g in range(max(GROUPS - 2, 0), GROUPS):
        out_copy(g).wait()
    total = own_sum[...]
    for off in range(1, tp):
        tp_copy(off).wait_recv()
        total = total + tp_in[off - 1]
    for off in range(1, tp):
        tp_copy(off).wait_send()
    sums[...] = total


def fused(queries, keys, values, gain, starts, source_unit):
    n = lax.axis_size("ctx")
    tp = lax.axis_size("tp")
    my_index = lax.axis_index("ctx")
    tokens, columns = queries.shape
    slots = CAP * n
    unit_rows = tokens // slots
    heads = columns // DH
    group_heads = heads // GROUPS
    blocks = tokens // BLK
    owners = source_unit.reshape(n, slots)
    source_shard = owners // slots
    source_slot = owners % slots
    earlier = jnp.arange(slots)[None, :] < jnp.arange(slots)[:, None]
    same_source = source_shard[:, :, None] == source_shard[:, None, :]
    rank = jnp.sum(jnp.where(same_source & earlier[None], 1, 0), axis=2).astype(jnp.int32)
    matches = (source_shard == my_index)[:, None, :] & (
        rank[:, None, :] == jnp.arange(CAP, dtype=jnp.int32)[None, :, None]
    )
    chosen = jnp.sum(jnp.where(matches, source_slot[:, None, :], 0), axis=2).reshape(-1)
    lookup = lax.dynamic_index_in_dim(source_shard * CAP + rank, my_index, 0, keepdims=False)
    doc = jnp.cumsum(starts).astype(jnp.int32)
    block_starts = starts.reshape(blocks, BLK)
    flags = jnp.stack(
        [jnp.where(jnp.any(block_starts > 0, axis=1), 0.0, 1.0),
         jnp.where(block_starts[:, 0] > 0, 0.0, 1.0)]
    ).astype(jnp.float32)
    doc_col = jnp.broadcast_to(doc[:, None], (tokens, DH))
    doc_row = jnp.broadcast_to(doc[None, :], (8, tokens))
    pieces = 3 * GROUPS
    piece = (slots, group_heads, unit_rows, DH)
    bf16, f32 = jnp.bfloat16, jnp.float32
    hbm = pl.BlockSpec(memory_space=pl.ANY)
    smem = pl.BlockSpec(memory_space=pltpu.SMEM)
    vmem = pl.BlockSpec(memory_space=pltpu.VMEM)
    ordered = pltpu.VMEM((group_heads, tokens, DH), bf16)
    dma = pltpu.SemaphoreType.DMA
    attended, sums = pl.pallas_call(
        functools.partial(exchange_kernel, n, tp),
        out_shape=(
            jax.ShapeDtypeStruct((tokens, columns), bf16),
            jax.ShapeDtypeStruct((8, tokens), f32),
        ),
        in_specs=[hbm, hbm, hbm, smem, smem, smem, vmem, vmem],
        out_specs=(hbm, vmem),
        scratch_shapes=[
            [pltpu.VMEM((slots, unit_rows, group_heads * DH), bf16) for _ in range(2)],
            pltpu.VMEM((pieces,) + piece, bf16),
            [pltpu.VMEM(piece, bf16) for _ in range(pieces)],
            ordered, ordered, ordered,
            pltpu.VMEM((GROUPS, group_heads, DH, DH), bf16),
            pltpu.VMEM((GROUPS, group_heads, DH, DH), bf16),
            pltpu.VMEM((GROUPS, blocks, group_heads, DH, DH), f32),
            pltpu.VMEM((2, tokens, group_heads * DH), bf16),
            pltpu.VMEM((tokens, DH), f32),
            pltpu.VMEM((8, tokens), f32),
            pltpu.VMEM((max(tp - 1, 1), 8, tokens), f32),
            dma((2,)),
            dma((pieces, n - 1)),
            dma((pieces, n - 1)),
            dma((GROUPS,)),
            dma((GROUPS,)),
            dma((2,)),
            dma((max(tp - 1, 1),)),
            dma((max(tp - 1, 1),)),
        ],
        compiler_params=pltpu.CompilerParams(
            collective_id=0, has_side_effects=True, vmem_limit_bytes=62 * 1024 * 1024
        ),
    )(
        queries.reshape(slots, unit_rows, columns),
        keys.reshape(slots, unit_rows, columns),
        values.reshape(slots, unit_rows, columns),
        chosen, lookup, flags, doc_col, doc_row,
    )
    mean_square = sums[0] / (columns * tp)
    scale = lax.rsqrt(mean_square + 1e-06)[:, None]
    return (attended.astype(f32) * scale * gain).astype(bf16)


def local(queries, keys, values, gain, starts, source_unit):
    shard_count = lax.axis_size("ctx")
    my_index = lax.axis_index("ctx")
    token_count, column_count = queries.shape
    slot_count = 2 * shard_count
    unit_rows = token_count // slot_count
    head_count = column_count // DH
    owners = source_unit.reshape(shard_count, slot_count)
    source_shard = owners // slot_count
    source_slot = owners % slot_count
    earlier_slot = jnp.arange(slot_count)[None, :] < jnp.arange(slot_count)[:, None]
    same_source = source_shard[:, :, None] == source_shard[:, None, :]
    arrival_rank = jnp.sum(jnp.where(same_source & earlier_slot[None], 1, 0), axis=2).astype(
        jnp.int32
    )
    from_me = source_shard == my_index
    matches = from_me[:, None, :] & (
        arrival_rank[:, None, :] == jnp.arange(CAP, dtype=jnp.int32)[None, :, None]
    )
    chosen = jnp.sum(jnp.where(matches, source_slot[:, None, :], 0), axis=2).reshape(-1)
    occupied = jnp.any(matches, axis=2).reshape(-1)

    def packed(array):
        pieces = array.reshape(slot_count, unit_rows, column_count)[chosen]
        pieces = jnp.where(occupied[:, None, None], pieces, jnp.zeros_like(pieces))
        return pieces.reshape(shard_count, CAP * unit_rows, column_count)

    arrived = (
        lax.all_to_all(packed(queries), "ctx", split_axis=0, concat_axis=0, tiled=True),
        lax.all_to_all(packed(keys), "ctx", split_axis=0, concat_axis=0, tiled=True),
        lax.all_to_all(packed(values), "ctx", split_axis=0, concat_axis=0, tiled=True),
    )
    my_source = lax.dynamic_index_in_dim(source_shard, my_index, 0, keepdims=False)
    my_rank = lax.dynamic_index_in_dim(arrival_rank, my_index, 0, keepdims=False)
    lookup = my_source * CAP + my_rank

    def unpacked(array):
        return array.reshape(shard_count * CAP, unit_rows, column_count)[lookup].reshape(
            token_count, column_count
        )

    block_count = token_count // BLK
    q_feat = (
        jax.nn.silu(unpacked(arrived[0]).astype(jnp.float32))
        .astype(jnp.bfloat16)
        .reshape(block_count, BLK, head_count, DH)
    )
    k_feat = (
        jax.nn.silu(unpacked(arrived[1]).astype(jnp.float32))
        .astype(jnp.bfloat16)
        .reshape(block_count, BLK, head_count, DH)
    )
    v_bal = unpacked(arrived[2]).reshape(block_count, BLK, head_count, DH)
    block_starts = starts.reshape(block_count, BLK)
    local_doc = jnp.cumsum(starts).reshape(block_count, BLK)
    last_doc = local_doc[:, BLK - 1 :]
    recent = jnp.where((local_doc == last_doc)[:, :, None, None], k_feat, jnp.zeros_like(k_feat))
    block_states = jnp.einsum("bshd,bshe->bhde", recent, v_bal, preferred_element_type=jnp.float32)
    has_start = jnp.any(block_starts > 0, axis=1)
    opening = block_starts[:, 0] > 0
    running = jnp.zeros((head_count, DH, DH), jnp.float32)
    for position in range(block_count):
        running = jnp.where(has_start[position], 0.0, running) + block_states[position]
    shard_flag = jnp.any(starts > 0).astype(jnp.float32).reshape(1)
    all_flags = lax.all_gather(shard_flag, "ctx", axis=0, tiled=True)
    shard_ids = jnp.arange(shard_count, dtype=jnp.int32)
    lowest = jnp.max(jnp.where((shard_ids < my_index) & (all_flags > 0), shard_ids, 0))
    piece = lax.all_gather(running[None], "ctx", axis=0, tiled=True)
    ids = jnp.arange(piece.shape[0], dtype=jnp.int32)
    wanted = (ids >= lowest) & (ids < my_index)
    incoming = jnp.sum(jnp.where(wanted[:, None, None, None], piece, 0.0), axis=0)
    causal = jnp.tril(jnp.ones((BLK, BLK), dtype=bool))
    scores = jnp.einsum("bthd,bshd->bhts", q_feat, k_feat, preferred_element_type=jnp.float32)
    allowed = causal[None] & (local_doc[:, :, None] == local_doc[:, None, :])
    weights = jnp.where(allowed[:, None], scores, 0.0).astype(jnp.bfloat16)
    within = jnp.einsum("bhts,bshe->bthe", weights, v_bal, preferred_element_type=jnp.float32)
    carry_state = incoming
    carried_parts = []
    for position in range(block_count):
        entering = jnp.where(opening[position], 0.0, carry_state).astype(jnp.bfloat16)
        carried = jnp.einsum(
            "thd,hde->the", q_feat[position], entering, preferred_element_type=jnp.float32
        )
        seen = local_doc[position] == local_doc[position, 0]
        carried_parts.append(jnp.where(seen[:, None, None], carried, 0.0))
        carry_state = jnp.where(has_start[position], 0.0, carry_state) + block_states[position]
    attended = jnp.stack(carried_parts) + within
    flat = attended.reshape(token_count, column_count)
    square_sums = lax.psum(jnp.sum(flat * flat, axis=1), "tp")
    mean_square = square_sums / (column_count * lax.axis_size("tp"))
    return (flat * lax.rsqrt(mean_square + 1e-06)[:, None] * gain).astype(jnp.bfloat16)


def solution(mesh):
    in_specs = (P("ctx", "tp"), P("ctx", "tp"), P("ctx", "tp"), P("tp"), P("ctx"), P())
    out_specs = P("ctx", "tp")

    def body(queries, keys, values, gain, starts, source_unit):
        unit_rows = queries.shape[0] // (CAP * mesh.shape["ctx"])
        whole = unit_rows % 16 == 0 and queries.shape[1] % (GROUPS * DH) == 0
        return (fused if whole else local)(queries, keys, values, gain, starts, source_unit)

    return jax.shard_map(body, mesh=mesh, in_specs=in_specs, out_specs=out_specs, check_vma=False)
```

```python
import functools
import jax
import jax.numpy as jnp
from jax import lax
from jax.experimental import pallas as pl
from jax.experimental.pallas import tpu as pltpu
from jax.sharding import PartitionSpec as P

DH = 128
CAP = 2
BLK = 768
TILE = 256
GROUPS = 8
WINDOW = 4
STAGGER = 8
MESH = pl.DeviceIdType.MESH


def silu(x):
    x = x.astype(jnp.float32)
    return (x / (1.0 + jnp.exp(-x))).astype(jnp.bfloat16)


def exchange_kernel(
    n, tp, q_in, k_in, v_in, chosen, lookup, flags, doc_col, doc_row,
    out, sums, staged, packed, arrived, q_ord, k_ord, v_ord, chain_in, chain_out, block_state,
    out_buf, squares, own_sum, tp_in,
    stage_sem, send_sem, recv_sem, chain_send, chain_recv, out_sem, tp_send, tp_recv,
):
    me = lax.axis_index("ctx")
    my_tp = lax.axis_index("tp")
    slots, unit_rows, _ = q_in.shape
    group_heads = q_ord.shape[0]
    width = group_heads * DH
    tokens = slots * unit_rows
    blocks = tokens // BLK
    sources = []
    for g in range(GROUPS):
        sources += [(k_in, g, True), (v_in, g, False)]
    sources += [(q_in, g, True) for g in range(GROUPS)]
    pieces = len(sources)

    def stage(i):
        ref, g, _ = sources[i]
        return pltpu.make_async_copy(
            ref.at[:, :, pl.ds(g * width, width)], staged[i % 2], stage_sem.at[i % 2]
        )

    def prepare(i):
        stage(i).wait()
        feature = sources[i][2]

        def one(u, _):
            rows = staged[i % 2][chosen[u]]
            rows = silu(rows) if feature else rows
            for h in range(group_heads):
                packed[i, u, h] = rows[:, h * DH : (h + 1) * DH]
            return 0

        lax.fori_loop(0, slots, one, 0)
        if i + 2 < pieces:
            stage(i + 2).start()
        mine = pl.ds(CAP * me, CAP)
        arrived[i][mine] = packed[i, mine]

    half = n // 2
    side, place = me // half, lax.rem(me, half)

    def remote(i, off):
        turn = lax.rem(off - 1 + lax.rem(my_tp, 2), n - 1)
        other = 1 - lax.rem(turn, 2)
        step = (turn + 1) // 2
        to = lax.rem(side + other, 2) * half + lax.rem(place + step, half)
        return pltpu.make_async_remote_copy(
            src_ref=packed.at[i, pl.ds(CAP * to, CAP)],
            dst_ref=arrived[i].at[pl.ds(CAP * me, CAP)],
            send_sem=send_sem.at[i, turn],
            recv_sem=recv_sem.at[i, turn],
            device_id={"ctx": to},
            device_id_type=MESH,
        )

    def each_peer(i, action):
        def one(off, _):
            action(remote(i, off))
            return 0

        lax.fori_loop(1, n, one, 0)

    def unpack(i, target):
        def one(u, _):
            rows = pl.ds(pl.multiple_of(u * unit_rows, unit_rows), unit_rows)
            target[:, rows, :] = arrived[i][lookup[u]]
            return 0

        lax.fori_loop(0, slots, one, 0)

    def chain(g):
        return pltpu.make_async_remote_copy(
            src_ref=chain_out.at[g],
            dst_ref=chain_in.at[g],
            send_sem=chain_send.at[g],
            recv_sem=chain_recv.at[g],
            device_id={"ctx": lax.rem(me + 1, n)},
            device_id_type=MESH,
        )

    def states(g):
        each_peer(2 * g, lambda c: c.wait_recv())
        each_peer(2 * g + 1, lambda c: c.wait_recv())
        unpack(2 * g, k_ord)
        unpack(2 * g + 1, v_ord)
        for b in range(blocks):
            rows = slice(b * BLK, (b + 1) * BLK)
            last = doc_col[(b + 1) * BLK - 1 : (b + 1) * BLK, :]
            recent = doc_col[rows, :] == last

            def one(h, _):
                keys = jnp.where(recent, k_ord[h, rows, :], 0.0).astype(jnp.bfloat16)
                block_state[g, b, h] = lax.dot_general(
                    keys, v_ord[h, rows, :], (((0,), (0,)), ((), ())),
                    preferred_element_type=jnp.float32,
                )
                return 0

            lax.fori_loop(0, group_heads, one, 0)

    def pass_on(g):
        @pl.when(me > 0)
        def _():
            chain(g).wait_recv()

        @pl.when(me < n - 1)
        def _():
            running = chain_in[g].astype(jnp.float32)
            for b in range(blocks):
                running = flags[0, b] * running + block_state[g, b]
            chain_out[g] = running.astype(jnp.bfloat16)
            chain(g).start()

    def out_copy(g):
        return pltpu.make_async_copy(
            out_buf.at[g % 2], out.at[:, pl.ds(g * width, width)], out_sem.at[g % 2]
        )

    def attend(g):
        each_peer(2 * GROUPS + g, lambda c: c.wait_recv())
        unpack(2 * GROUPS + g, q_ord)
        unpack(2 * g, k_ord)
        unpack(2 * g + 1, v_ord)
        if g >= 2:
            out_copy(g - 2).wait()
        for b in range(blocks):
            for t in range(BLK // TILE):
                first = b * BLK
                rows = slice(first + t * TILE, first + (t + 1) * TILE)
                keys = slice(first, first + (t + 1) * TILE)
                span = (t + 1) * TILE
                here = doc_col[rows, :]
                causal = lax.broadcasted_iota(jnp.int32, (TILE, span), 1) <= (
                    lax.broadcasted_iota(jnp.int32, (TILE, span), 0) + t * TILE
                )
                allowed = causal & (here[:, :1] == doc_row[:1, keys])
                seen = here == doc_col[first : first + 1, :]

                def one(h, _):
                    running = chain_in[g, h].astype(jnp.float32)
                    for p in range(b):
                        running = flags[0, p] * running + block_state[g, p, h]
                    entering = (flags[1, b] * running).astype(jnp.bfloat16)
                    query = q_ord[h, rows, :]
                    scores = lax.dot_general(
                        query, k_ord[h, keys, :], (((1,), (1,)), ((), ())),
                        preferred_element_type=jnp.float32,
                    )
                    weights = jnp.where(allowed, scores, 0.0).astype(jnp.bfloat16)
                    within = jnp.dot(
                        weights, v_ord[h, keys, :], preferred_element_type=jnp.float32
                    )
                    carried = jnp.dot(query, entering, preferred_element_type=jnp.float32)
                    total = within + jnp.where(seen, carried, 0.0)
                    squares[rows, :] += total * total
                    columns = pl.ds(pl.multiple_of(h * DH, DH), DH)
                    out_buf[g % 2, rows, columns] = total.astype(jnp.bfloat16)
                    return 0

                lax.fori_loop(0, group_heads, one, 0)
        out_copy(g).start()

    def tp_copy(off):
        return pltpu.make_async_remote_copy(
            src_ref=own_sum,
            dst_ref=tp_in.at[off - 1],
            send_sem=tp_send.at[off - 1],
            recv_sem=tp_recv.at[off - 1],
            device_id={"tp": lax.rem(my_tp + off, tp)},
            device_id_type=MESH,
        )

    def follow(done):
        if 0 <= done < 2 * GROUPS and done % 2 == 1:
            states(done // 2)
        if 1 <= done < 2 * GROUPS + STAGGER:
            late = done - 1 - me * STAGGER // n

            @pl.when((late >= 0) & (lax.rem(late, 2) == 0) & (late < 2 * GROUPS))
            def _():
                pass_on(late // 2)

        if done >= 2 * GROUPS:
            attend(done - 2 * GROUPS)

    barrier = pltpu.get_barrier_semaphore()
    stage(0).start()
    stage(1).start()

    def greet_ctx(off, _):
        pl.semaphore_signal(
            barrier, inc=1, device_id={"ctx": lax.rem(me + off, n)}, device_id_type=MESH
        )
        return 0

    def greet_tp(off, _):
        pl.semaphore_signal(
            barrier, inc=1, device_id={"tp": lax.rem(my_tp + off, tp)}, device_id_type=MESH
        )
        return 0

    lax.fori_loop(1, n, greet_ctx, 0)
    lax.fori_loop(1, tp, greet_tp, 0)
    prepare(0)
    pl.semaphore_wait(barrier, n - 1 + tp - 1)
    squares[...] = jnp.zeros_like(squares)

    @pl.when(me == 0)
    def _():
        chain_in[...] = jnp.zeros_like(chain_in)


    for i in range(pieces):
        if i > 0:
            prepare(i)
        if i >= WINDOW:
            each_peer(i - WINDOW, lambda c: c.wait_send())
        each_peer(i, lambda c: c.start())
        follow(i - WINDOW)
    for i in range(pieces - WINDOW, pieces):
        follow(i)
    own_sum[...] = lax.dot_general(
        jnp.ones((8, DH), jnp.float32), squares[...], (((1,), (1,)), ((), ())),
        preferred_element_type=jnp.float32, precision=lax.Precision.HIGHEST,
    )
    for off in range(1, tp):
        tp_copy(off).start()
    for i in range(pieces - WINDOW, pieces):
        each_peer(i, lambda c: c.wait_send())

    @pl.when(me < n - 1)
    def _():
        for g in range(GROUPS):
            chain(g).wait_send()

    for g in range(max(GROUPS - 2, 0), GROUPS):
        out_copy(g).wait()
    total = own_sum[...]
    for off in range(1, tp):
        tp_copy(off).wait_recv()
        total = total + tp_in[off - 1]
    for off in range(1, tp):
        tp_copy(off).wait_send()
    sums[...] = total


def fused(queries, keys, values, gain, starts, source_unit):
    n = lax.axis_size("ctx")
    tp = lax.axis_size("tp")
    my_index = lax.axis_index("ctx")
    tokens, columns = queries.shape
    slots = CAP * n
    unit_rows = tokens // slots
    heads = columns // DH
    group_heads = heads // GROUPS
    blocks = tokens // BLK
    owners = source_unit.reshape(n, slots)
    source_shard = owners // slots
    source_slot = owners % slots
    earlier = jnp.arange(slots)[None, :] < jnp.arange(slots)[:, None]
    same_source = source_shard[:, :, None] == source_shard[:, None, :]
    rank = jnp.sum(jnp.where(same_source & earlier[None], 1, 0), axis=2).astype(jnp.int32)
    matches = (source_shard == my_index)[:, None, :] & (
        rank[:, None, :] == jnp.arange(CAP, dtype=jnp.int32)[None, :, None]
    )
    chosen = jnp.sum(jnp.where(matches, source_slot[:, None, :], 0), axis=2).reshape(-1)
    lookup = lax.dynamic_index_in_dim(source_shard * CAP + rank, my_index, 0, keepdims=False)
    doc = jnp.cumsum(starts).astype(jnp.int32)
    block_starts = starts.reshape(blocks, BLK)
    flags = jnp.stack(
        [jnp.where(jnp.any(block_starts > 0, axis=1), 0.0, 1.0),
         jnp.where(block_starts[:, 0] > 0, 0.0, 1.0)]
    ).astype(jnp.float32)
    doc_col = jnp.broadcast_to(doc[:, None], (tokens, DH))
    doc_row = jnp.broadcast_to(doc[None, :], (8, tokens))
    pieces = 3 * GROUPS
    piece = (slots, group_heads, unit_rows, DH)
    bf16, f32 = jnp.bfloat16, jnp.float32
    hbm = pl.BlockSpec(memory_space=pl.ANY)
    smem = pl.BlockSpec(memory_space=pltpu.SMEM)
    vmem = pl.BlockSpec(memory_space=pltpu.VMEM)
    ordered = pltpu.VMEM((group_heads, tokens, DH), bf16)
    dma = pltpu.SemaphoreType.DMA
    attended, sums = pl.pallas_call(
        functools.partial(exchange_kernel, n, tp),
        out_shape=(
            jax.ShapeDtypeStruct((tokens, columns), bf16),
            jax.ShapeDtypeStruct((8, tokens), f32),
        ),
        in_specs=[hbm, hbm, hbm, smem, smem, smem, vmem, vmem],
        out_specs=(hbm, vmem),
        scratch_shapes=[
            [pltpu.VMEM((slots, unit_rows, group_heads * DH), bf16) for _ in range(2)],
            pltpu.VMEM((pieces,) + piece, bf16),
            [pltpu.VMEM(piece, bf16) for _ in range(pieces)],
            ordered, ordered, ordered,
            pltpu.VMEM((GROUPS, group_heads, DH, DH), bf16),
            pltpu.VMEM((GROUPS, group_heads, DH, DH), bf16),
            pltpu.VMEM((GROUPS, blocks, group_heads, DH, DH), f32),
            pltpu.VMEM((2, tokens, group_heads * DH), bf16),
            pltpu.VMEM((tokens, DH), f32),
            pltpu.VMEM((8, tokens), f32),
            pltpu.VMEM((max(tp - 1, 1), 8, tokens), f32),
            dma((2,)),
            dma((pieces, n - 1)),
            dma((pieces, n - 1)),
            dma((GROUPS,)),
            dma((GROUPS,)),
            dma((2,)),
            dma((max(tp - 1, 1),)),
            dma((max(tp - 1, 1),)),
        ],
        compiler_params=pltpu.CompilerParams(
            collective_id=0, has_side_effects=True, vmem_limit_bytes=62 * 1024 * 1024
        ),
    )(
        queries.reshape(slots, unit_rows, columns),
        keys.reshape(slots, unit_rows, columns),
        values.reshape(slots, unit_rows, columns),
        chosen, lookup, flags, doc_col, doc_row,
    )
    mean_square = sums[0] / (columns * tp)
    scale = lax.rsqrt(mean_square + 1e-06)[:, None]
    return (attended.astype(f32) * scale * gain).astype(bf16)


def local(queries, keys, values, gain, starts, source_unit):
    shard_count = lax.axis_size("ctx")
    my_index = lax.axis_index("ctx")
    token_count, column_count = queries.shape
    slot_count = 2 * shard_count
    unit_rows = token_count // slot_count
    head_count = column_count // DH
    owners = source_unit.reshape(shard_count, slot_count)
    source_shard = owners // slot_count
    source_slot = owners % slot_count
    earlier_slot = jnp.arange(slot_count)[None, :] < jnp.arange(slot_count)[:, None]
    same_source = source_shard[:, :, None] == source_shard[:, None, :]
    arrival_rank = jnp.sum(jnp.where(same_source & earlier_slot[None], 1, 0), axis=2).astype(
        jnp.int32
    )
    from_me = source_shard == my_index
    matches = from_me[:, None, :] & (
        arrival_rank[:, None, :] == jnp.arange(CAP, dtype=jnp.int32)[None, :, None]
    )
    chosen = jnp.sum(jnp.where(matches, source_slot[:, None, :], 0), axis=2).reshape(-1)
    occupied = jnp.any(matches, axis=2).reshape(-1)

    def packed(array):
        pieces = array.reshape(slot_count, unit_rows, column_count)[chosen]
        pieces = jnp.where(occupied[:, None, None], pieces, jnp.zeros_like(pieces))
        return pieces.reshape(shard_count, CAP * unit_rows, column_count)

    arrived = (
        lax.all_to_all(packed(queries), "ctx", split_axis=0, concat_axis=0, tiled=True),
        lax.all_to_all(packed(keys), "ctx", split_axis=0, concat_axis=0, tiled=True),
        lax.all_to_all(packed(values), "ctx", split_axis=0, concat_axis=0, tiled=True),
    )
    my_source = lax.dynamic_index_in_dim(source_shard, my_index, 0, keepdims=False)
    my_rank = lax.dynamic_index_in_dim(arrival_rank, my_index, 0, keepdims=False)
    lookup = my_source * CAP + my_rank

    def unpacked(array):
        return array.reshape(shard_count * CAP, unit_rows, column_count)[lookup].reshape(
            token_count, column_count
        )

    block_count = token_count // BLK
    q_feat = (
        jax.nn.silu(unpacked(arrived[0]).astype(jnp.float32))
        .astype(jnp.bfloat16)
        .reshape(block_count, BLK, head_count, DH)
    )
    k_feat = (
        jax.nn.silu(unpacked(arrived[1]).astype(jnp.float32))
        .astype(jnp.bfloat16)
        .reshape(block_count, BLK, head_count, DH)
    )
    v_bal = unpacked(arrived[2]).reshape(block_count, BLK, head_count, DH)
    block_starts = starts.reshape(block_count, BLK)
    local_doc = jnp.cumsum(starts).reshape(block_count, BLK)
    last_doc = local_doc[:, BLK - 1 :]
    recent = jnp.where((local_doc == last_doc)[:, :, None, None], k_feat, jnp.zeros_like(k_feat))
    block_states = jnp.einsum("bshd,bshe->bhde", recent, v_bal, preferred_element_type=jnp.float32)
    has_start = jnp.any(block_starts > 0, axis=1)
    opening = block_starts[:, 0] > 0
    running = jnp.zeros((head_count, DH, DH), jnp.float32)
    for position in range(block_count):
        running = jnp.where(has_start[position], 0.0, running) + block_states[position]
    shard_flag = jnp.any(starts > 0).astype(jnp.float32).reshape(1)
    all_flags = lax.all_gather(shard_flag, "ctx", axis=0, tiled=True)
    shard_ids = jnp.arange(shard_count, dtype=jnp.int32)
    lowest = jnp.max(jnp.where((shard_ids < my_index) & (all_flags > 0), shard_ids, 0))
    piece = lax.all_gather(running[None], "ctx", axis=0, tiled=True)
    ids = jnp.arange(piece.shape[0], dtype=jnp.int32)
    wanted = (ids >= lowest) & (ids < my_index)
    incoming = jnp.sum(jnp.where(wanted[:, None, None, None], piece, 0.0), axis=0)
    causal = jnp.tril(jnp.ones((BLK, BLK), dtype=bool))
    scores = jnp.einsum("bthd,bshd->bhts", q_feat, k_feat, preferred_element_type=jnp.float32)
    allowed = causal[None] & (local_doc[:, :, None] == local_doc[:, None, :])
    weights = jnp.where(allowed[:, None], scores, 0.0).astype(jnp.bfloat16)
    within = jnp.einsum("bhts,bshe->bthe", weights, v_bal, preferred_element_type=jnp.float32)
    carry_state = incoming
    carried_parts = []
    for position in range(block_count):
        entering = jnp.where(opening[position], 0.0, carry_state).astype(jnp.bfloat16)
        carried = jnp.einsum(
            "thd,hde->the", q_feat[position], entering, preferred_element_type=jnp.float32
        )
        seen = local_doc[position] == local_doc[position, 0]
        carried_parts.append(jnp.where(seen[:, None, None], carried, 0.0))
        carry_state = jnp.where(has_start[position], 0.0, carry_state) + block_states[position]
    attended = jnp.stack(carried_parts) + within
    flat = attended.reshape(token_count, column_count)
    square_sums = lax.psum(jnp.sum(flat * flat, axis=1), "tp")
    mean_square = square_sums / (column_count * lax.axis_size("tp"))
    return (flat * lax.rsqrt(mean_square + 1e-06)[:, None] * gain).astype(jnp.bfloat16)


def solution(mesh):
    in_specs = (P("ctx", "tp"), P("ctx", "tp"), P("ctx", "tp"), P("tp"), P("ctx"), P())
    out_specs = P("ctx", "tp")

    def body(queries, keys, values, gain, starts, source_unit):
        unit_rows = queries.shape[0] // (CAP * mesh.shape["ctx"])
        whole = unit_rows % 16 == 0 and queries.shape[1] % (GROUPS * DH) == 0
        return (fused if whole else local)(queries, keys, values, gain, starts, source_unit)

    return jax.shard_map(body, mesh=mesh, in_specs=in_specs, out_specs=out_specs, check_vma=False)
```
